32 devices in a mesh: grp: 2 (over x), gx: 8 (over z, y), yz: 2 (over core).
Axes of the slice: x: 2, y: 2, z: 4, core: 2. Of those that a mesh axis runs over, the one named last changes fastest.
Arguments:
- start: float32 [2, 2, 3, 32, 128, 128], P(None, None, None, ('grp', 'gx'), 'yz'), parts along dimension 3, may hold values from -6 to 6
- masses: float32 [2, 32, 128, 128], P(None, ('grp', 'gx'), 'yz'), parts along dimension 1, may hold values from 0.8 to 1.25
- bond_long: float32 [4, 32, 128, 128], P(None, ('grp', 'gx'), 'yz'), parts along dimension 1, may hold values from 0.5 to 1.5
- bond_trans: float32 [4, 32, 128, 128], P(None, ('grp', 'gx'), 'yz'), parts along dimension 1, may hold values from 0.1 to 0.5
Outputs:
- last_vector: float32 [2, 2, 3, 32, 128, 128], P(None, None, None, ('grp', 'gx'), 'yz'), parts along dimension 3
- density: float32 [4, 2, 32, 128, 128], P(None, None, ('grp', 'gx'), 'yz'), parts along dimension 2
The draws below stay inside these ranges and needn't reach their ends.
There are 2 independent parts, one for each index of `grp`. The reference program is written for one: setup_inputs(seed, part) draws one part's arguments, and reference() takes and returns one part's arrays. A program takes and returns all parts, laid end to end along the dimension named above; each array names one. Nothing has to cross between parts.
All inputs are finite; a program needn't handle non-finite values.
Results may differ from the reference program's by a relative error of at most 0.0001.
Values sent between devices are 32-bit elements; how exact they have to be, the bound alone decides.
A program may use at most 64 MiB of HBM per device.

```python
import math
import jax
import jax.numpy as jnp
from jax import lax

NZ = 128
VECS = 2
STEPS = 4
NX = 16
NY = 128


def shard_levels(key, extent, cuts, smallest, high):
    gain, own = 1.0, jax.random.fold_in(key, 6)
    for position, shards_of in cuts:
        steps = jnp.exp(jax.random.uniform(jax.random.fold_in(own, position), (shards_of,), jnp.float32, smallest / len(cuts), high / len(cuts)))
        gain = gain * jnp.repeat(steps, extent[position] // shards_of).reshape([-1 if axis == position else 1 for axis in range(len(extent))])
    return gain


def noise(own_key, shape, spread, limit, split=(), kind=jnp.bfloat16):
    drawn = jax.random.normal(own_key, shape, jnp.float32) * spread
    if len(split) > 0:
        drawn = shard_levels(own_key, shape, split, -0.22, 0.18) * drawn
    return jnp.clip(drawn, min=-limit, max=limit).astype(kind)


def setup_inputs(seed: int = 0, part: int = 0) -> dict:
    key_list = jax.random.split(jax.random.key(seed), 5)
    part_keys = jax.random.split(jax.random.fold_in(key_list[4], part), 5)
    return {
        "start": noise(part_keys[0], (VECS, 2, 3, NX, NY, NZ), 1.0, 6.0, ((3, 8), (4, 2)), jnp.float32),
        "masses": jnp.clip(0.8 + 0.45 * jax.random.uniform(part_keys[1], (2, NX, NY, NZ), jnp.float32) ** shard_levels(part_keys[1], (2, NX, NY, NZ), ((1, 8), (2, 2)), -0.2, 0.2), 0.8, 1.25),
        "bond_long": jnp.clip(jnp.exp(math.log(1.5) - 1.0986123 * jax.random.uniform(part_keys[2], (4, NX, NY, NZ), jnp.float32) ** shard_levels(part_keys[2], (4, NX, NY, NZ), ((1, 8), (2, 2)), -0.2, 0.2)), 0.5, 1.5),
        "bond_trans": jnp.clip(jnp.exp(math.log(0.5) - 1.609438 * jax.random.uniform(part_keys[3], (4, NX, NY, NZ), jnp.float32) ** shard_levels(part_keys[3], (4, NX, NY, NZ), ((1, 8), (2, 2)), -0.2, 0.2)), 0.1, 0.5),
    }


root_third = 0.5773502691896258
bond_signs = [[1.0, 1.0, 1.0], [1.0, -1.0, -1.0], [-1.0, 1.0, -1.0], [-1.0, -1.0, 1.0]]
width_scale = 8.0

def bond_force(diff, stiff_long, stiff_trans, which):
    signs = bond_signs[which]
    along = (diff[:, 0] * signs[0] + diff[:, 1] * signs[1] + diff[:, 2] * signs[2]) * root_third
    extra = (stiff_long - stiff_trans) * along
    parts = [extra * (signs[comp] * root_third) for comp in range(3)]
    return stiff_trans * diff + jnp.stack(parts, axis=1)

def apply_operator(field, scale, bond_long, bond_trans):
    moved = field * scale[None, :, None]
    upper_a = moved[:, 0]
    upper_b = moved[:, 1]
    force_a = jnp.zeros_like(upper_a)
    force_b = jnp.zeros_like(upper_b)
    for which in range(4):
        if which == 0:
            lower = upper_b
        else:
            lower = jnp.roll(upper_b, 1, axis=which + 1)
        term = bond_force(upper_a - lower, bond_long[which], bond_trans[which], which)
        force_a = force_a + term
        if which == 0:
            force_b = force_b - term
        else:
            force_b = force_b - jnp.roll(term, -1, axis=which + 1)
    forces = jnp.stack([force_a, force_b], axis=1)
    return forces * scale[None, :, None] / width_scale - field

def reference(start, masses, bond_long, bond_trans):
    scale = 1.0 / jnp.sqrt(masses)
    before = start
    current = apply_operator(start, scale, bond_long, bond_trans)
    moments = [lax.optimization_barrier(jnp.sum(start * current, axis=(0, 2)))]
    for order in range(2, STEPS + 1):
        following = 2.0 * apply_operator(current, scale, bond_long, bond_trans) - before
        before = current
        current = following
        moments.append(lax.optimization_barrier(jnp.sum(start * current, axis=(0, 2))))
    return (current, jnp.stack(moments))
```

```python
import functools

import jax
import jax.numpy as jnp
from jax import lax
from jax.experimental import pallas as pl
from jax.experimental.pallas import tpu as pltpu
from jax.sharding import PartitionSpec as P

STEPS = 4
SIGNS = ((1, 1, 1), (1, -1, -1), (-1, 1, -1), (-1, -1, 1))
MESH = pl.DeviceIdType.MESH


def signed(x, sign, y):
    return x + y if sign > 0 else x - y


def add_bond(total, upper, lower, trans, extra, which):
    signs = SIGNS[which]
    diff = [upper[c] - lower[c] for c in range(3)]
    along = signed(signed(diff[0], signs[0] * signs[1], diff[1]), signs[0] * signs[2], diff[2])
    along = extra * along
    for c in range(3):
        part = trans * diff[c]
        part = signed(part, signs[c] * signs[0], along)
        total[c] = part if total[c] is None else total[c] + part
    return total


def kernel(
    ring, start_hbm, mass_hbm, long_hbm, trans_hbm, last_hbm, dens_hbm,
    start, mass, long, trans, scale, tran_a, extr_a, tran_b, extr_b,
    u, t, dens, halo, row_out, row_in, bond_in, rowbond_out, rowbond_in,
    load_sem, save_sem, x_send, x_recv, row_send, row_recv, bond_send, bond_recv, rowbond_send, rowbond_recv,
):
    vecs, _, _, planes, rows, lanes = start.shape
    me = lax.axis_index("gx")
    core = lax.axis_index("yz")
    right, left = lax.rem(me + 1, ring), lax.rem(me + ring - 1, ring)
    other = 1 - core

    loads = [
        pltpu.make_async_copy(src, dst, load_sem.at[i])
        for i, (src, dst) in enumerate(
            ((mass_hbm, mass), (start_hbm, start), (long_hbm, long), (trans_hbm, trans))
        )
    ]
    for load in loads:
        load.start()

    barrier = pltpu.get_barrier_semaphore()
    for target in ({"gx": left}, {"gx": right}, {"yz": other}):
        pl.semaphore_signal(barrier, inc=1, device_id=target, device_id_type=MESH)

    row_index = lax.broadcasted_iota(jnp.int32, (rows, lanes), 0)
    first_row, last_row = row_index == 0, row_index == rows - 1

    def x_copy(n, v, side):
        src = u.at[n, v, 1, planes - 1] if side == 0 else u.at[n, v, 0, 0]
        return pltpu.make_async_remote_copy(
            src_ref=src, dst_ref=halo.at[n, v, side],
            send_sem=x_send.at[n, v, side], recv_sem=x_recv.at[n, v, side],
            device_id={"gx": right if side == 0 else left}, device_id_type=MESH,
        )

    def row_copy(n, v):
        return pltpu.make_async_remote_copy(
            src_ref=row_out.at[n, v], dst_ref=row_in.at[n, v],
            send_sem=row_send.at[n, v], recv_sem=row_recv.at[n, v],
            device_id={"yz": other}, device_id_type=MESH,
        )

    def bond_copy(i):
        src = (long_hbm, trans_hbm)[i]
        return pltpu.make_async_remote_copy(
            src_ref=src.at[1, 0], dst_ref=bond_in.at[i],
            send_sem=bond_send.at[i], recv_sem=bond_recv.at[i],
            device_id={"gx": left}, device_id_type=MESH,
        )

    rowbond_copy = pltpu.make_async_remote_copy(
        src_ref=rowbond_out, dst_ref=rowbond_in, send_sem=rowbond_send, recv_sem=rowbond_recv,
        device_id={"yz": other}, device_id_type=MESH,
    )

    def put_rows(n, v, sub, plane):
        edge = 0 if sub == 0 else rows - 1
        for c in range(3):
            row_out[n, v, sub, plane * 3 + c] = u[n, v, sub, plane, c, edge]

    def first_u(v, sub, plane):
        for c in range(3):
            u[0, v, sub, plane, c] = scale[sub, plane] * start[v, sub, c, plane]
        put_rows(0, v, sub, plane)

    loads[0].wait()
    scale[...] = lax.rsqrt(mass[...])
    loads[1].wait()
    first_u(0, 1, planes - 1)
    first_u(0, 0, 0)
    pl.semaphore_wait(barrier, 3)
    x_copy(0, 0, 0).start()
    x_copy(0, 0, 1).start()
    for i in range(2):
        bond_copy(i).start()
    first_u(1, 1, planes - 1)
    first_u(1, 0, 0)
    for v in range(1, vecs):
        x_copy(0, v, 0).start()
        x_copy(0, v, 1).start()
    for v in range(vecs):
        for plane in range(planes - 1):
            first_u(v, 1, plane)
            first_u(v, 0, plane + 1)
        row_copy(0, v).start()

    loads[2].wait()
    loads[3].wait()

    def scaled_extra(stiff_long, stiff_trans):
        return (stiff_long - stiff_trans) * (1.0 / 24.0)

    for plane in range(planes):
        for b in range(4):
            tran_a[b, plane] = trans[b, plane] * 0.125
            extr_a[b, plane] = scaled_extra(long[b, plane], trans[b, plane])
        rowbond_out[plane] = tran_a[2, plane, 0]
        rowbond_out[planes + plane] = extr_a[2, plane, 0]
    rowbond_copy.start()
    for plane in range(planes):
        for i, (coef_a, coef_b) in enumerate(((tran_a, tran_b), (extr_a, extr_b))):
            coef_b[1, plane] = pltpu.roll(coef_a[3, plane], lanes - 1, 1)
    rowbond_copy.wait_recv()
    for plane in range(planes):
        for i, (coef_a, coef_b) in enumerate(((tran_a, tran_b), (extr_a, extr_b))):
            turned = pltpu.roll(coef_a[2, plane], rows - 1, 0)
            edge = rowbond_in[i * planes + plane].reshape(1, lanes)
            coef_b[0, plane] = jnp.where(last_row, edge, turned)

    def update(n, v, sub, plane):
        own = [u[n, v, sub, plane, c] for c in range(3)]
        near = [u[n, v, 1 - sub, plane, c] for c in range(3)]
        if sub == 0:
            beside = [halo[n, v, 0, c] if plane == 0 else u[n, v, 1, plane - 1, c] for c in range(3)]
        else:
            beside = [halo[n, v, 1, c] if plane == planes - 1 else u[n, v, 0, plane + 1, c] for c in range(3)]
        edges = [row_in[n, v, 1 - sub, plane * 3 + c].reshape(1, lanes) for c in range(3)]
        shift, at_edge = (1, first_row) if sub == 0 else (rows - 1, last_row)
        along_y = [jnp.where(at_edge, edges[c], pltpu.roll(near[c], shift, 0)) for c in range(3)]
        along_z = [pltpu.roll(near[c], 1 if sub == 0 else lanes - 1, 1) for c in range(3)]
        total = [None] * 3
        for b, far in enumerate((near, beside, along_y, along_z)):
            if sub == 0 or b == 0:
                coef = tran_a[b, plane], extr_a[b, plane]
            elif b == 1 and plane == planes - 1:
                coef = bond_in[2], bond_in[3]
            elif b == 1:
                coef = tran_a[1, plane + 1], extr_a[1, plane + 1]
            else:
                coef = tran_b[b - 2, plane], extr_b[b - 2, plane]
            total = add_bond(total, own, far, *coef, b)
        own_scale = scale[sub, plane]
        gain = own_scale if n == 0 else own_scale + own_scale
        moment = None
        for c in range(3):
            first = start[v, sub, c, plane]
            now = first if n == 0 else t[n - 1, v, sub, c, plane]
            new = gain * total[c]
            if n == 0:
                new = new - now
            else:
                before = first if n == 1 else t[n - 2, v, sub, c, plane]
                new = new - (now + now) - before
            t[n, v, sub, c, plane] = new
            if n < STEPS - 1:
                u[n + 1, v, sub, plane, c] = own_scale * new
            moment = first * new if moment is None else moment + first * new
        if v == 0:
            dens[n, sub, plane] = moment
        else:
            dens[n, sub, plane] += moment
        if n < STEPS - 1:
            put_rows(n + 1, v, sub, plane)

    saves = []
    for n in range(STEPS):
        for v in range(vecs):
            row_copy(n, v).wait_recv()
            for plane in range(planes - 1):
                update(n, v, 0, plane + 1)
                update(n, v, 1, plane)
            x_copy(n, v, 0).wait_recv()
            update(n, v, 0, 0)
            if n < STEPS - 1:
                x_copy(n + 1, v, 1).start()
            x_copy(n, v, 1).wait_recv()
            if n == 0 and v == 0:
                for i in range(2):
                    bond_copy(i).wait_recv()
                bond_in[2] = bond_in[1] * 0.125
                bond_in[3] = scaled_extra(bond_in[0], bond_in[1])
            update(n, v, 1, planes - 1)
            if n < STEPS - 1:
                x_copy(n + 1, v, 0).start()
                row_copy(n + 1, v).start()
            else:
                saves.append(pltpu.make_async_copy(t.at[n, v], last_hbm.at[v], save_sem.at[STEPS + v]))
                saves[-1].start()
        saves.append(pltpu.make_async_copy(dens.at[n], dens_hbm.at[n], save_sem.at[n]))
        saves[-1].start()

    for n in range(STEPS):
        for v in range(vecs):
            row_copy(n, v).wait_send()
            for side in range(2):
                x_copy(n, v, side).wait_send()
    for i in range(2):
        bond_copy(i).wait_send()
    rowbond_copy.wait_send()
    for save in saves:
        save.wait()


def on_device(ring, start, masses, bond_long, bond_trans):
    vecs, _, _, planes, rows, lanes = start.shape
    f32 = jnp.float32
    plane = (rows, lanes)
    vmem = lambda *shape: pltpu.VMEM(shape, f32)
    dma = lambda *shape: pltpu.SemaphoreType.DMA(shape)
    padded = -(-3 * planes // 8) * 8
    padded_bonds = -(-2 * planes // 8) * 8
    return pl.pallas_call(
        functools.partial(kernel, ring),
        out_shape=(
            jax.ShapeDtypeStruct(start.shape, f32),
            jax.ShapeDtypeStruct((STEPS, 2, planes, rows, lanes), f32),
        ),
        in_specs=[pl.BlockSpec(memory_space=pl.ANY)] * 4,
        out_specs=(pl.BlockSpec(memory_space=pl.ANY),) * 2,
        scratch_shapes=[
            vmem(*start.shape), vmem(*masses.shape), vmem(*bond_long.shape), vmem(*bond_trans.shape),
            vmem(*masses.shape),
            vmem(4, planes, *plane), vmem(4, planes, *plane), vmem(2, planes, *plane), vmem(2, planes, *plane),
            vmem(STEPS, vecs, 2, planes, 3, *plane),
            vmem(STEPS, *start.shape),
            vmem(STEPS, 2, planes, *plane),
            vmem(STEPS, vecs, 2, 3, *plane),
            vmem(STEPS, vecs, 2, padded, lanes), vmem(STEPS, vecs, 2, padded, lanes),
            vmem(4, *plane),
            vmem(padded_bonds, lanes), vmem(padded_bonds, lanes),
            dma(4), dma(STEPS + vecs),
            dma(STEPS, vecs, 2), dma(STEPS, vecs, 2), dma(STEPS, vecs), dma(STEPS, vecs),
            dma(2), dma(2), pltpu.SemaphoreType.DMA, pltpu.SemaphoreType.DMA,
        ],
        compiler_params=pltpu.CompilerParams(
            collective_id=0, has_side_effects=True, vmem_limit_bytes=32 * 1024 * 1024
        ),
        name="chebyshev",
    )(start, masses, bond_long, bond_trans)


def solution(mesh):
    in_specs = (
        P(None, None, None, ("grp", "gx"), "yz", None),
        P(None, ("grp", "gx"), "yz", None),
        P(None, ("grp", "gx"), "yz", None),
        P(None, ("grp", "gx"), "yz", None),
    )
    out_specs = (
        P(None, None, None, ("grp", "gx"), "yz", None),
        P(None, None, ("grp", "gx"), "yz", None),
    )
    return jax.shard_map(
        functools.partial(on_device, mesh.shape["gx"]),
        mesh=mesh, in_specs=in_specs, out_specs=out_specs, check_vma=False,
    )
```

```python
import functools

import jax
import jax.numpy as jnp
from jax import lax
from jax.experimental import pallas as pl
from jax.experimental.pallas import tpu as pltpu
from jax.sharding import PartitionSpec as P

STEPS = 4
SIGNS = ((1, 1, 1), (1, -1, -1), (-1, 1, -1), (-1, -1, 1))
MESH = pl.DeviceIdType.MESH


def signed(x, sign, y):
    return x + y if sign > 0 else x - y


def add_bond(total, upper, lower, trans, extra, which):
    signs = SIGNS[which]
    diff = [upper[c] - lower[c] for c in range(3)]
    along = signed(signed(diff[0], signs[0] * signs[1], diff[1]), signs[0] * signs[2], diff[2])
    along = extra * along
    for c in range(3):
        part = trans * diff[c]
        part = signed(part, signs[c] * signs[0], along)
        total[c] = part if total[c] is None else total[c] + part
    return total


def kernel(
    ring, start_hbm, mass_hbm, long_hbm, trans_hbm, last, dens,
    start, mass, long, trans, scale, tran_a, extr_a, tran_b, extr_b,
    u, t, halo, row_out, row_in, bond_in, rowbond_out, rowbond_in,
    load_sem, x_send, x_recv, row_send, row_recv, bond_send, bond_recv, rowbond_send, rowbond_recv,
):
    vecs, _, _, planes, rows, lanes = start.shape
    me = lax.axis_index("gx")
    core = lax.axis_index("yz")
    right, left = lax.rem(me + 1, ring), lax.rem(me + ring - 1, ring)
    other = 1 - core

    loads = [
        pltpu.make_async_copy(src, dst, load_sem.at[i])
        for i, (src, dst) in enumerate(
            ((mass_hbm, mass), (start_hbm, start), (long_hbm, long), (trans_hbm, trans))
        )
    ]
    for load in loads:
        load.start()

    barrier = pltpu.get_barrier_semaphore()
    for target in ({"gx": left}, {"gx": right}, {"yz": other}):
        pl.semaphore_signal(barrier, inc=1, device_id=target, device_id_type=MESH)

    row_index = lax.broadcasted_iota(jnp.int32, (rows, lanes), 0)
    first_row, last_row = row_index == 0, row_index == rows - 1

    def x_copy(n, v, side):
        src = u.at[n, v, 1, planes - 1] if side == 0 else u.at[n, v, 0, 0]
        return pltpu.make_async_remote_copy(
            src_ref=src, dst_ref=halo.at[n, v, side],
            send_sem=x_send.at[n, v, side], recv_sem=x_recv.at[n, v, side],
            device_id={"gx": right if side == 0 else left}, device_id_type=MESH,
        )

    def row_copy(n, v):
        return pltpu.make_async_remote_copy(
            src_ref=row_out.at[n, v], dst_ref=row_in.at[n, v],
            send_sem=row_send.at[n, v], recv_sem=row_recv.at[n, v],
            device_id={"yz": other}, device_id_type=MESH,
        )

    def bond_copy(i):
        src = (long_hbm, trans_hbm)[i]
        return pltpu.make_async_remote_copy(
            src_ref=src.at[1, 0], dst_ref=bond_in.at[i],
            send_sem=bond_send.at[i], recv_sem=bond_recv.at[i],
            device_id={"gx": left}, device_id_type=MESH,
        )

    rowbond_copy = pltpu.make_async_remote_copy(
        src_ref=rowbond_out, dst_ref=rowbond_in, send_sem=rowbond_send, recv_sem=rowbond_recv,
        device_id={"yz": other}, device_id_type=MESH,
    )

    def put_rows(n, v, sub, plane):
        edge = 0 if sub == 0 else rows - 1
        for c in range(3):
            row_out[n, v, sub, plane * 3 + c] = u[n, v, sub, plane, c, edge]

    def first_u(v, sub, plane):
        for c in range(3):
            u[0, v, sub, plane, c] = scale[sub, plane] * start[v, sub, c, plane]
        put_rows(0, v, sub, plane)

    loads[0].wait()
    scale[...] = lax.rsqrt(mass[...])
    loads[1].wait()
    first_u(0, 1, planes - 1)
    first_u(0, 0, 0)
    pl.semaphore_wait(barrier, 3)
    x_copy(0, 0, 0).start()
    x_copy(0, 0, 1).start()
    for i in range(2):
        bond_copy(i).start()
    first_u(1, 1, planes - 1)
    first_u(1, 0, 0)
    for v in range(1, vecs):
        x_copy(0, v, 0).start()
        x_copy(0, v, 1).start()
    for v in range(vecs):
        for plane in range(planes - 1):
            first_u(v, 1, plane)
            first_u(v, 0, plane + 1)
        row_copy(0, v).start()

    loads[2].wait()
    loads[3].wait()

    def scaled_extra(stiff_long, stiff_trans):
        return (stiff_long - stiff_trans) * (1.0 / 24.0)

    for plane in range(planes):
        for b in range(4):
            tran_a[b, plane] = trans[b, plane] * 0.125
            extr_a[b, plane] = scaled_extra(long[b, plane], trans[b, plane])
        rowbond_out[plane] = tran_a[2, plane, 0]
        rowbond_out[planes + plane] = extr_a[2, plane, 0]
    rowbond_copy.start()
    for plane in range(planes):
        for i, (coef_a, coef_b) in enumerate(((tran_a, tran_b), (extr_a, extr_b))):
            coef_b[1, plane] = pltpu.roll(coef_a[3, plane], lanes - 1, 1)
    rowbond_copy.wait_recv()
    for plane in range(planes):
        for i, (coef_a, coef_b) in enumerate(((tran_a, tran_b), (extr_a, extr_b))):
            turned = pltpu.roll(coef_a[2, plane], rows - 1, 0)
            edge = rowbond_in[i * planes + plane].reshape(1, lanes)
            coef_b[0, plane] = jnp.where(last_row, edge, turned)

    def update(n, v, sub, plane):
        own = [u[n, v, sub, plane, c] for c in range(3)]
        near = [u[n, v, 1 - sub, plane, c] for c in range(3)]
        if sub == 0:
            beside = [halo[n, v, 0, c] if plane == 0 else u[n, v, 1, plane - 1, c] for c in range(3)]
        else:
            beside = [halo[n, v, 1, c] if plane == planes - 1 else u[n, v, 0, plane + 1, c] for c in range(3)]
        edges = [row_in[n, v, 1 - sub, plane * 3 + c].reshape(1, lanes) for c in range(3)]
        shift, at_edge = (1, first_row) if sub == 0 else (rows - 1, last_row)
        along_y = [jnp.where(at_edge, edges[c], pltpu.roll(near[c], shift, 0)) for c in range(3)]
        along_z = [pltpu.roll(near[c], 1 if sub == 0 else lanes - 1, 1) for c in range(3)]
        total = [None] * 3
        for b, far in enumerate((near, beside, along_y, along_z)):
            if sub == 0 or b == 0:
                coef = tran_a[b, plane], extr_a[b, plane]
            elif b == 1 and plane == planes - 1:
                coef = bond_in[2], bond_in[3]
            elif b == 1:
                coef = tran_a[1, plane + 1], extr_a[1, plane + 1]
            else:
                coef = tran_b[b - 2, plane], extr_b[b - 2, plane]
            total = add_bond(total, own, far, *coef, b)
        own_scale = scale[sub, plane]
        gain = own_scale if n == 0 else own_scale + own_scale
        moment = None
        for c in range(3):
            first = start[v, sub, c, plane]
            now = first if n == 0 else t[n - 1, v, sub, c, plane]
            new = gain * total[c]
            if n == 0:
                new = new - now
            else:
                before = first if n == 1 else t[n - 2, v, sub, c, plane]
                new = new - (now + now) - before
            if n == STEPS - 1:
                last[v, sub, c, plane] = new
            else:
                t[n, v, sub, c, plane] = new
                u[n + 1, v, sub, plane, c] = own_scale * new
            moment = first * new if moment is None else moment + first * new
        if v == 0:
            dens[n, sub, plane] = moment
        else:
            dens[n, sub, plane] += moment
        if n < STEPS - 1:
            put_rows(n + 1, v, sub, plane)

    for n in range(STEPS):
        for v in range(vecs):
            row_copy(n, v).wait_recv()
            for plane in range(planes - 1):
                update(n, v, 0, plane + 1)
                update(n, v, 1, plane)
            x_copy(n, v, 0).wait_recv()
            update(n, v, 0, 0)
            if n < STEPS - 1:
                x_copy(n + 1, v, 1).start()
            x_copy(n, v, 1).wait_recv()
            if n == 0 and v == 0:
                for i in range(2):
                    bond_copy(i).wait_recv()
                bond_in[2] = bond_in[1] * 0.125
                bond_in[3] = scaled_extra(bond_in[0], bond_in[1])
            update(n, v, 1, planes - 1)
            if n < STEPS - 1:
                x_copy(n + 1, v, 0).start()
                row_copy(n + 1, v).start()

    for n in range(STEPS):
        for v in range(vecs):
            row_copy(n, v).wait_send()
            for side in range(2):
                x_copy(n, v, side).wait_send()
    for i in range(2):
        bond_copy(i).wait_send()
    rowbond_copy.wait_send()


def on_device(ring, start, masses, bond_long, bond_trans):
    vecs, _, _, planes, rows, lanes = start.shape
    f32 = jnp.float32
    plane = (rows, lanes)
    vmem = lambda *shape: pltpu.VMEM(shape, f32)
    dma = lambda *shape: pltpu.SemaphoreType.DMA(shape)
    padded = -(-3 * planes // 8) * 8
    padded_bonds = -(-2 * planes // 8) * 8
    return pl.pallas_call(
        functools.partial(kernel, ring),
        out_shape=(
            jax.ShapeDtypeStruct(start.shape, f32),
            jax.ShapeDtypeStruct((STEPS, 2, planes, rows, lanes), f32),
        ),
        in_specs=[pl.BlockSpec(memory_space=pltpu.HBM)] * 4,
        out_specs=(pl.BlockSpec(memory_space=pltpu.VMEM),) * 2,
        scratch_shapes=[
            vmem(*start.shape), vmem(*masses.shape), vmem(*bond_long.shape), vmem(*bond_trans.shape),
            vmem(*masses.shape),
            vmem(4, planes, *plane), vmem(4, planes, *plane), vmem(2, planes, *plane), vmem(2, planes, *plane),
            vmem(STEPS, vecs, 2, planes, 3, *plane),
            vmem(STEPS - 1, *start.shape),
            vmem(STEPS, vecs, 2, 3, *plane),
            vmem(STEPS, vecs, 2, padded, lanes), vmem(STEPS, vecs, 2, padded, lanes),
            vmem(4, *plane),
            vmem(padded_bonds, lanes), vmem(padded_bonds, lanes),
            dma(4),
            dma(STEPS, vecs, 2), dma(STEPS, vecs, 2), dma(STEPS, vecs), dma(STEPS, vecs),
            dma(2), dma(2), pltpu.SemaphoreType.DMA, pltpu.SemaphoreType.DMA,
        ],
        compiler_params=pltpu.CompilerParams(
            collective_id=0, has_side_effects=True, vmem_limit_bytes=32 * 1024 * 1024
        ),
        name="chebyshev",
    )(*(pltpu.with_memory_space_constraint(x, pltpu.HBM) for x in (start, masses, bond_long, bond_trans)))


def solution(mesh):
    in_specs = (
        P(None, None, None, ("grp", "gx"), "yz", None),
        P(None, ("grp", "gx"), "yz", None),
        P(None, ("grp", "gx"), "yz", None),
        P(None, ("grp", "gx"), "yz", None),
    )
    out_specs = (
        P(None, None, None, ("grp", "gx"), "yz", None),
        P(None, None, ("grp", "gx"), "yz", None),
    )
    return jax.shard_map(
        functools.partial(on_device, mesh.shape["gx"]),
        mesh=mesh, in_specs=in_specs, out_specs=out_specs, check_vma=False,
    )
```

```python
import functools

import jax
import jax.numpy as jnp
from jax import lax
from jax.experimental import pallas as pl
from jax.experimental.pallas import tpu as pltpu
from jax.sharding import PartitionSpec as P

STEPS = 4
SIGNS = ((1, 1, 1), (1, -1, -1), (-1, 1, -1), (-1, -1, 1))
MESH = pl.DeviceIdType.MESH


def signed(x, sign, y):
    return x + y if sign > 0 else x - y


def add_bond(total, upper, lower, trans, extra, which):
    signs = SIGNS[which]
    diff = [upper[c] - lower[c] for c in range(3)]
    along = signed(signed(diff[0], signs[0] * signs[1], diff[1]), signs[0] * signs[2], diff[2])
    along = extra * along
    for c in range(3):
        part = trans * diff[c]
        part = signed(part, signs[c] * signs[0], along)
        total[c] = part if total[c] is None else total[c] + part
    return total


def kernel(
    ring, start_hbm, mass_hbm, long_hbm, trans_hbm, last, dens,
    start, mass, long, trans, scale, tran_a, extr_a, tran_b, extr_b,
    u, t, halo, row_out, row_in, bond_in, rowbond_out, rowbond_in,
    load_sem, x_send, x_recv, row_send, row_recv, bond_send, bond_recv, rowbond_send, rowbond_recv,
):
    vecs, _, _, planes, rows, lanes = start.shape
    me = lax.axis_index("gx")
    core = lax.axis_index("yz")
    right, left = lax.rem(me + 1, ring), lax.rem(me + ring - 1, ring)
    other = 1 - core

    loads = [
        pltpu.make_async_copy(src, dst, load_sem.at[i])
        for i, (src, dst) in enumerate(
            ((mass_hbm, mass), (start_hbm, start), (long_hbm, long), (trans_hbm, trans))
        )
    ]
    for load in loads[:2]:
        load.start()

    barrier = pltpu.get_barrier_semaphore()
    for target in ({"gx": left}, {"gx": right}, {"yz": other}):
        pl.semaphore_signal(barrier, inc=1, device_id=target, device_id_type=MESH)

    row_index = lax.broadcasted_iota(jnp.int32, (rows, lanes), 0)
    first_row, last_row = row_index == 0, row_index == rows - 1

    def x_copy(n, v, side):
        src = u.at[n, v, 1, planes - 1] if side == 0 else u.at[n, v, 0, 0]
        return pltpu.make_async_remote_copy(
            src_ref=src, dst_ref=halo.at[n, v, side],
            send_sem=x_send.at[n, v, side], recv_sem=x_recv.at[n, v, side],
            device_id={"gx": right if side == 0 else left}, device_id_type=MESH,
        )

    def row_copy(n, v):
        return pltpu.make_async_remote_copy(
            src_ref=row_out.at[n, v], dst_ref=row_in.at[n, v],
            send_sem=row_send.at[n, v], recv_sem=row_recv.at[n, v],
            device_id={"yz": other}, device_id_type=MESH,
        )

    def bond_copy(i):
        src = (long_hbm, trans_hbm)[i]
        return pltpu.make_async_remote_copy(
            src_ref=src.at[1, 0], dst_ref=bond_in.at[i],
            send_sem=bond_send.at[i], recv_sem=bond_recv.at[i],
            device_id={"gx": left}, device_id_type=MESH,
        )

    rowbond_copy = pltpu.make_async_remote_copy(
        src_ref=rowbond_out, dst_ref=rowbond_in, send_sem=rowbond_send, recv_sem=rowbond_recv,
        device_id={"yz": other}, device_id_type=MESH,
    )

    def put_rows(n, v, sub, plane):
        edge = 0 if sub == 0 else rows - 1
        for c in range(3):
            row_out[n, v, sub, plane * 3 + c] = u[n, v, sub, plane, c, edge]

    def first_u(v, sub, plane):
        for c in range(3):
            u[0, v, sub, plane, c] = scale[sub, plane] * start[v, sub, c, plane]
        put_rows(0, v, sub, plane)

    pl.semaphore_wait(barrier, 3)
    for i in range(2):
        bond_copy(i).start()
    for load in loads[2:]:
        load.start()
    loads[0].wait()
    scale[...] = lax.rsqrt(mass[...])
    loads[1].wait()
    first_u(0, 1, planes - 1)
    x_copy(0, 0, 0).start()
    first_u(0, 0, 0)
    x_copy(0, 0, 1).start()
    first_u(1, 1, planes - 1)
    first_u(1, 0, 0)
    for v in range(1, vecs):
        x_copy(0, v, 0).start()
        x_copy(0, v, 1).start()
    for v in range(vecs):
        for plane in range(planes - 1):
            first_u(v, 1, plane)
            first_u(v, 0, plane + 1)
        row_copy(0, v).start()

    loads[2].wait()
    loads[3].wait()

    def scaled_extra(stiff_long, stiff_trans):
        return (stiff_long - stiff_trans) * (1.0 / 24.0)

    for plane in range(planes):
        for b in range(4):
            tran_a[b, plane] = trans[b, plane] * 0.125
            extr_a[b, plane] = scaled_extra(long[b, plane], trans[b, plane])
        rowbond_out[plane] = tran_a[2, plane, 0]
        rowbond_out[planes + plane] = extr_a[2, plane, 0]
    rowbond_copy.start()
    for plane in range(planes):
        for i, (coef_a, coef_b) in enumerate(((tran_a, tran_b), (extr_a, extr_b))):
            coef_b[1, plane] = pltpu.roll(coef_a[3, plane], lanes - 1, 1)
    rowbond_copy.wait_recv()
    for plane in range(planes):
        for i, (coef_a, coef_b) in enumerate(((tran_a, tran_b), (extr_a, extr_b))):
            turned = pltpu.roll(coef_a[2, plane], rows - 1, 0)
            edge = rowbond_in[i * planes + plane].reshape(1, lanes)
            coef_b[0, plane] = jnp.where(last_row, edge, turned)

    def update(n, v, sub, plane):
        own = [u[n, v, sub, plane, c] for c in range(3)]
        near = [u[n, v, 1 - sub, plane, c] for c in range(3)]
        if sub == 0:
            beside = [halo[n, v, 0, c] if plane == 0 else u[n, v, 1, plane - 1, c] for c in range(3)]
        else:
            beside = [halo[n, v, 1, c] if plane == planes - 1 else u[n, v, 0, plane + 1, c] for c in range(3)]
        edges = [row_in[n, v, 1 - sub, plane * 3 + c].reshape(1, lanes) for c in range(3)]
        shift, at_edge = (1, first_row) if sub == 0 else (rows - 1, last_row)
        along_y = [jnp.where(at_edge, edges[c], pltpu.roll(near[c], shift, 0)) for c in range(3)]
        along_z = [pltpu.roll(near[c], 1 if sub == 0 else lanes - 1, 1) for c in range(3)]
        total = [None] * 3
        for b, far in enumerate((near, beside, along_y, along_z)):
            if sub == 0 or b == 0:
                coef = tran_a[b, plane], extr_a[b, plane]
            elif b == 1 and plane == planes - 1:
                coef = bond_in[2], bond_in[3]
            elif b == 1:
                coef = tran_a[1, plane + 1], extr_a[1, plane + 1]
            else:
                coef = tran_b[b - 2, plane], extr_b[b - 2, plane]
            total = add_bond(total, own, far, *coef, b)
        own_scale = scale[sub, plane]
        gain = own_scale if n == 0 else own_scale + own_scale
        moment = None
        for c in range(3):
            first = start[v, sub, c, plane]
            now = first if n == 0 else t[n - 1, v, sub, c, plane]
            new = gain * total[c]
            if n == 0:
                new = new - now
            else:
                before = first if n == 1 else t[n - 2, v, sub, c, plane]
                new = new - (now + now) - before
            if n == STEPS - 1:
                last[v, sub, c, plane] = new
            else:
                t[n, v, sub, c, plane] = new
                u[n + 1, v, sub, plane, c] = own_scale * new
            moment = first * new if moment is None else moment + first * new
        if v == 0:
            dens[n, sub, plane] = moment
        else:
            dens[n, sub, plane] += moment
        if n < STEPS - 1:
            put_rows(n + 1, v, sub, plane)

    for n in range(STEPS):
        for v in range(vecs):
            row_copy(n, v).wait_recv()
            for plane in range(planes - 1):
                update(n, v, 0, plane + 1)
                update(n, v, 1, plane)
            x_copy(n, v, 0).wait_recv()
            update(n, v, 0, 0)
            if n < STEPS - 1:
                x_copy(n + 1, v, 1).start()
            x_copy(n, v, 1).wait_recv()
            if n == 0 and v == 0:
                for i in range(2):
                    bond_copy(i).wait_recv()
                bond_in[2] = bond_in[1] * 0.125
                bond_in[3] = scaled_extra(bond_in[0], bond_in[1])
            update(n, v, 1, planes - 1)
            if n < STEPS - 1:
                x_copy(n + 1, v, 0).start()
                row_copy(n + 1, v).start()

    for n in range(STEPS):
        for v in range(vecs):
            row_copy(n, v).wait_send()
            for side in range(2):
                x_copy(n, v, side).wait_send()
    for i in range(2):
        bond_copy(i).wait_send()
    rowbond_copy.wait_send()


def flush_kernel(last_in, dens_in, last_out, dens_out, sem):
    pairs = [(src.at[i], dst.at[i]) for src, dst in ((last_in, last_out), (dens_in, dens_out)) for i in range(src.shape[0])]
    copies = [pltpu.make_async_copy(src, dst, sem.at[i]) for i, (src, dst) in enumerate(pairs)]
    for copy in copies:
        copy.start()
    for copy in copies:
        copy.wait()


def flush(last, dens):
    return pl.pallas_call(
        flush_kernel,
        out_shape=tuple(jax.ShapeDtypeStruct(x.shape, x.dtype) for x in (last, dens)),
        in_specs=[pl.BlockSpec(memory_space=pl.ANY)] * 2,
        out_specs=(pl.BlockSpec(memory_space=pl.ANY),) * 2,
        scratch_shapes=[pltpu.SemaphoreType.DMA((last.shape[0] + dens.shape[0],))],
        name="flush",
    )(*(pltpu.with_memory_space_constraint(x, pltpu.VMEM) for x in (last, dens)))


def on_device(ring, start, masses, bond_long, bond_trans):
    vecs, _, _, planes, rows, lanes = start.shape
    f32 = jnp.float32
    plane = (rows, lanes)
    vmem = lambda *shape: pltpu.VMEM(shape, f32)
    dma = lambda *shape: pltpu.SemaphoreType.DMA(shape)
    padded = -(-3 * planes // 8) * 8
    padded_bonds = -(-2 * planes // 8) * 8
    last, dens = pl.pallas_call(
        functools.partial(kernel, ring),
        out_shape=(
            jax.ShapeDtypeStruct(start.shape, f32),
            jax.ShapeDtypeStruct((STEPS, 2, planes, rows, lanes), f32),
        ),
        in_specs=[pl.BlockSpec(memory_space=pltpu.HBM)] * 4,
        out_specs=(pl.BlockSpec(memory_space=pltpu.VMEM),) * 2,
        scratch_shapes=[
            vmem(*start.shape), vmem(*masses.shape), vmem(*bond_long.shape), vmem(*bond_trans.shape),
            vmem(*masses.shape),
            vmem(4, planes, *plane), vmem(4, planes, *plane), vmem(2, planes, *plane), vmem(2, planes, *plane),
            vmem(STEPS, vecs, 2, planes, 3, *plane),
            vmem(STEPS - 1, *start.shape),
            vmem(STEPS, vecs, 2, 3, *plane),
            vmem(STEPS, vecs, 2, padded, lanes), vmem(STEPS, vecs, 2, padded, lanes),
            vmem(4, *plane),
            vmem(padded_bonds, lanes), vmem(padded_bonds, lanes),
            dma(4),
            dma(STEPS, vecs, 2), dma(STEPS, vecs, 2), dma(STEPS, vecs), dma(STEPS, vecs),
            dma(2), dma(2), pltpu.SemaphoreType.DMA, pltpu.SemaphoreType.DMA,
        ],
        compiler_params=pltpu.CompilerParams(
            collective_id=0, has_side_effects=True, vmem_limit_bytes=32 * 1024 * 1024
        ),
        name="chebyshev",
    )(*(pltpu.with_memory_space_constraint(x, pltpu.HBM) for x in (start, masses, bond_long, bond_trans)))
    return flush(last, dens)


def solution(mesh):
    in_specs = (
        P(None, None, None, ("grp", "gx"), "yz", None),
        P(None, ("grp", "gx"), "yz", None),
        P(None, ("grp", "gx"), "yz", None),
        P(None, ("grp", "gx"), "yz", None),
    )
    out_specs = (
        P(None, None, None, ("grp", "gx"), "yz", None),
        P(None, None, ("grp", "gx"), "yz", None),
    )
    return jax.shard_map(
        functools.partial(on_device, mesh.shape["gx"]),
        mesh=mesh, in_specs=in_specs, out_specs=out_specs, check_vma=False,
    )
```

```python
import functools

import jax
import jax.numpy as jnp
from jax import lax
from jax.experimental import pallas as pl
from jax.experimental.pallas import tpu as pltpu
from jax.sharding import PartitionSpec as P

STEPS = 4
SIGNS = ((1, 1, 1), (1, -1, -1), (-1, 1, -1), (-1, -1, 1))
MESH = pl.DeviceIdType.MESH


def signed(x, sign, y):
    return x + y if sign > 0 else x - y


def add_bond(total, upper, lower, trans, extra, which):
    signs = SIGNS[which]
    diff = [upper[c] - lower[c] for c in range(3)]
    along = signed(signed(diff[0], signs[0] * signs[1], diff[1]), signs[0] * signs[2], diff[2])
    along = extra * along
    for c in range(3):
        part = trans * diff[c]
        part = signed(part, signs[c] * signs[0], along)
        total[c] = part if total[c] is None else total[c] + part
    return total


def kernel(
    ring, start_hbm, mass_hbm, long_hbm, trans_hbm, last, dens,
    start, mass, long, trans, scale, tran_a, extr_a, tran_b, extr_b,
    u, t, halo, row_out, row_in, bond_in, rowbond_out, rowbond_in,
    load_sem, x_send, x_recv, row_send, row_recv, bond_send, bond_recv, rowbond_send, rowbond_recv,
):
    vecs, _, _, planes, rows, lanes = start.shape
    me = lax.axis_index("gx")
    core = lax.axis_index("yz")
    right, left = lax.rem(me + 1, ring), lax.rem(me + ring - 1, ring)
    other = 1 - core

    loads = [
        pltpu.make_async_copy(src, dst, load_sem.at[i])
        for i, (src, dst) in enumerate(
            ((mass_hbm, mass), (start_hbm, start), (long_hbm, long), (trans_hbm, trans))
        )
    ]
    for load in loads[:2]:
        load.start()

    barrier = pltpu.get_barrier_semaphore()
    for target in ({"gx": left}, {"gx": right}, {"yz": other}):
        pl.semaphore_signal(barrier, inc=1, device_id=target, device_id_type=MESH)

    row_index = lax.broadcasted_iota(jnp.int32, (rows, lanes), 0)
    first_row, last_row = row_index == 0, row_index == rows - 1

    def x_copy(n, v, side):
        src = u.at[n, v, 1, planes - 1] if side == 0 else u.at[n, v, 0, 0]
        return pltpu.make_async_remote_copy(
            src_ref=src, dst_ref=halo.at[n, v, side],
            send_sem=x_send.at[n, v, side], recv_sem=x_recv.at[n, v, side],
            device_id={"gx": right if side == 0 else left}, device_id_type=MESH,
        )

    def row_copy(n, v):
        return pltpu.make_async_remote_copy(
            src_ref=row_out.at[n, v], dst_ref=row_in.at[n, v],
            send_sem=row_send.at[n, v], recv_sem=row_recv.at[n, v],
            device_id={"yz": other}, device_id_type=MESH,
        )

    def bond_copy(i):
        src = (long_hbm, trans_hbm)[i]
        return pltpu.make_async_remote_copy(
            src_ref=src.at[1, 0], dst_ref=bond_in.at[i],
            send_sem=bond_send.at[i], recv_sem=bond_recv.at[i],
            device_id={"gx": left}, device_id_type=MESH,
        )

    rowbond_copy = pltpu.make_async_remote_copy(
        src_ref=rowbond_out, dst_ref=rowbond_in, send_sem=rowbond_send, recv_sem=rowbond_recv,
        device_id={"yz": other}, device_id_type=MESH,
    )

    def put_rows(n, v, sub, plane):
        edge = 0 if sub == 0 else rows - 1
        for c in range(3):
            row_out[n, v, sub, plane * 3 + c] = u[n, v, sub, plane, c, edge]

    def first_u(v, sub, plane):
        for c in range(3):
            u[0, v, sub, plane, c] = scale[sub, plane] * start[v, sub, c, plane]
        put_rows(0, v, sub, plane)

    pl.semaphore_wait(barrier, 3)
    for i in range(2):
        bond_copy(i).start()
    for load in loads[2:]:
        load.start()
    loads[0].wait()
    scale[...] = lax.rsqrt(mass[...])
    loads[1].wait()
    first_u(0, 1, planes - 1)
    x_copy(0, 0, 0).start()
    first_u(0, 0, 0)
    x_copy(0, 0, 1).start()
    first_u(1, 1, planes - 1)
    first_u(1, 0, 0)
    for v in range(1, vecs):
        x_copy(0, v, 0).start()
        x_copy(0, v, 1).start()
    for v in range(vecs):
        for plane in range(planes - 1):
            first_u(v, 1, plane)
            first_u(v, 0, plane + 1)
        row_copy(0, v).start()

    loads[2].wait()
    loads[3].wait()

    def scaled_extra(stiff_long, stiff_trans):
        return (stiff_long - stiff_trans) * (1.0 / 24.0)

    for plane in range(planes):
        for b in range(4):
            tran_a[b, plane] = trans[b, plane] * 0.125
            extr_a[b, plane] = scaled_extra(long[b, plane], trans[b, plane])
        rowbond_out[plane] = tran_a[2, plane, 0]
        rowbond_out[planes + plane] = extr_a[2, plane, 0]
    rowbond_copy.start()
    for plane in range(planes):
        for i, (coef_a, coef_b) in enumerate(((tran_a, tran_b), (extr_a, extr_b))):
            coef_b[1, plane] = pltpu.roll(coef_a[3, plane], lanes - 1, 1)
    rowbond_copy.wait_recv()
    for plane in range(planes):
        for i, (coef_a, coef_b) in enumerate(((tran_a, tran_b), (extr_a, extr_b))):
            turned = pltpu.roll(coef_a[2, plane], rows - 1, 0)
            edge = rowbond_in[i * planes + plane].reshape(1, lanes)
            coef_b[0, plane] = jnp.where(last_row, edge, turned)

    def update(n, v, sub, plane):
        own = [u[n, v, sub, plane, c] for c in range(3)]
        near = [u[n, v, 1 - sub, plane, c] for c in range(3)]
        if sub == 0:
            beside = [halo[n, v, 0, c] if plane == 0 else u[n, v, 1, plane - 1, c] for c in range(3)]
        else:
            beside = [halo[n, v, 1, c] if plane == planes - 1 else u[n, v, 0, plane + 1, c] for c in range(3)]
        edges = [row_in[n, v, 1 - sub, plane * 3 + c].reshape(1, lanes) for c in range(3)]
        shift, at_edge = (1, first_row) if sub == 0 else (rows - 1, last_row)
        along_y = [jnp.where(at_edge, edges[c], pltpu.roll(near[c], shift, 0)) for c in range(3)]
        along_z = [pltpu.roll(near[c], 1 if sub == 0 else lanes - 1, 1) for c in range(3)]
        total = [None] * 3
        for b, far in enumerate((near, beside, along_y, along_z)):
            if sub == 0 or b == 0:
                coef = tran_a[b, plane], extr_a[b, plane]
            elif b == 1 and plane == planes - 1:
                coef = bond_in[2], bond_in[3]
            elif b == 1:
                coef = tran_a[1, plane + 1], extr_a[1, plane + 1]
            else:
                coef = tran_b[b - 2, plane], extr_b[b - 2, plane]
            total = add_bond(total, own, far, *coef, b)
        own_scale = scale[sub, plane]
        gain = own_scale if n == 0 else own_scale + own_scale
        moment = None
        for c in range(3):
            first = start[v, sub, c, plane]
            now = first if n == 0 else t[n - 1, v, sub, c, plane]
            new = gain * total[c]
            if n == 0:
                new = new - now
            else:
                before = first if n == 1 else t[n - 2, v, sub, c, plane]
                new = new - (now + now) - before
            if n == STEPS - 1:
                last[v, sub, c, plane] = new
            else:
                t[n, v, sub, c, plane] = new
                u[n + 1, v, sub, plane, c] = own_scale * new
            moment = first * new if moment is None else moment + first * new
        if v == 0:
            dens[n, sub, plane] = moment
        else:
            dens[n, sub, plane] += moment
        if n < STEPS - 1:
            put_rows(n + 1, v, sub, plane)

    for n in range(STEPS):
        for v in range(vecs):
            row_copy(n, v).wait_recv()
            x_copy(n, v, 0).wait_recv()
            update(n, v, 0, 0)
            if n < STEPS - 1:
                x_copy(n + 1, v, 1).start()
            x_copy(n, v, 1).wait_recv()
            if n == 0 and v == 0:
                for i in range(2):
                    bond_copy(i).wait_recv()
                bond_in[2] = bond_in[1] * 0.125
                bond_in[3] = scaled_extra(bond_in[0], bond_in[1])
            update(n, v, 1, planes - 1)
            if n < STEPS - 1:
                x_copy(n + 1, v, 0).start()
            for plane in range(planes - 1):
                update(n, v, 0, plane + 1)
                update(n, v, 1, plane)
            if n < STEPS - 1:
                row_copy(n + 1, v).start()

    for n in range(STEPS):
        for v in range(vecs):
            row_copy(n, v).wait_send()
            for side in range(2):
                x_copy(n, v, side).wait_send()
    for i in range(2):
        bond_copy(i).wait_send()
    rowbond_copy.wait_send()


def flush_kernel(last_in, dens_in, last_out, dens_out, sem):
    pairs = [(src.at[i], dst.at[i]) for src, dst in ((last_in, last_out), (dens_in, dens_out)) for i in range(src.shape[0])]
    copies = [pltpu.make_async_copy(src, dst, sem.at[i]) for i, (src, dst) in enumerate(pairs)]
    for copy in copies:
        copy.start()
    for copy in copies:
        copy.wait()


def flush(last, dens):
    return pl.pallas_call(
        flush_kernel,
        out_shape=tuple(jax.ShapeDtypeStruct(x.shape, x.dtype) for x in (last, dens)),
        in_specs=[pl.BlockSpec(memory_space=pl.ANY)] * 2,
        out_specs=(pl.BlockSpec(memory_space=pl.ANY),) * 2,
        scratch_shapes=[pltpu.SemaphoreType.DMA((last.shape[0] + dens.shape[0],))],
        name="flush",
    )(*(pltpu.with_memory_space_constraint(x, pltpu.VMEM) for x in (last, dens)))


def on_device(ring, start, masses, bond_long, bond_trans):
    vecs, _, _, planes, rows, lanes = start.shape
    f32 = jnp.float32
    plane = (rows, lanes)
    vmem = lambda *shape: pltpu.VMEM(shape, f32)
    dma = lambda *shape: pltpu.SemaphoreType.DMA(shape)
    padded = -(-3 * planes // 8) * 8
    padded_bonds = -(-2 * planes // 8) * 8
    last, dens = pl.pallas_call(
        functools.partial(kernel, ring),
        out_shape=(
            jax.ShapeDtypeStruct(start.shape, f32),
            jax.ShapeDtypeStruct((STEPS, 2, planes, rows, lanes), f32),
        ),
        in_specs=[pl.BlockSpec(memory_space=pltpu.HBM)] * 4,
        out_specs=(pl.BlockSpec(memory_space=pltpu.VMEM),) * 2,
        scratch_shapes=[
            vmem(*start.shape), vmem(*masses.shape), vmem(*bond_long.shape), vmem(*bond_trans.shape),
            vmem(*masses.shape),
            vmem(4, planes, *plane), vmem(4, planes, *plane), vmem(2, planes, *plane), vmem(2, planes, *plane),
            vmem(STEPS, vecs, 2, planes, 3, *plane),
            vmem(STEPS - 1, *start.shape),
            vmem(STEPS, vecs, 2, 3, *plane),
            vmem(STEPS, vecs, 2, padded, lanes), vmem(STEPS, vecs, 2, padded, lanes),
            vmem(4, *plane),
            vmem(padded_bonds, lanes), vmem(padded_bonds, lanes),
            dma(4),
            dma(STEPS, vecs, 2), dma(STEPS, vecs, 2), dma(STEPS, vecs), dma(STEPS, vecs),
            dma(2), dma(2), pltpu.SemaphoreType.DMA, pltpu.SemaphoreType.DMA,
        ],
        compiler_params=pltpu.CompilerParams(
            collective_id=0, has_side_effects=True, vmem_limit_bytes=32 * 1024 * 1024
        ),
        name="chebyshev",
    )(*(pltpu.with_memory_space_constraint(x, pltpu.HBM) for x in (start, masses, bond_long, bond_trans)))
    return flush(last, dens)


def solution(mesh):
    in_specs = (
        P(None, None, None, ("grp", "gx"), "yz", None),
        P(None, ("grp", "gx"), "yz", None),
        P(None, ("grp", "gx"), "yz", None),
        P(None, ("grp", "gx"), "yz", None),
    )
    out_specs = (
        P(None, None, None, ("grp", "gx"), "yz", None),
        P(None, None, ("grp", "gx"), "yz", None),
    )
    return jax.shard_map(
        functools.partial(on_device, mesh.shape["gx"]),
        mesh=mesh, in_specs=in_specs, out_specs=out_specs, check_vma=False,
    )
```
